32 devices in a mesh: fsdp: 8 (over z, y), owner: 4 (over x, core).
Axes of the slice: x: 2, y: 2, z: 4, core: 2. Of those that a mesh axis runs over, the one named last changes fastest.
Arguments:
- grads: bfloat16 [32, 1024, 1024], P(None, ('fsdp', 'owner'))
- second_moment: float32 [32, 1024, 1024], P(None, ('fsdp', 'owner')), may hold values from 0.00024414062 to 0.00390625
- assign: int32 [32], replicated, may hold values from 0 to 31, each once
- left_stats: float32 [32, 1024, 1024], P(('fsdp', 'owner')), as said below
- right_stats: float32 [32, 1024, 1024], P(('fsdp', 'owner')), as said below
Outputs:
- update: bfloat16 [32, 1024, 1024], P(None, ('fsdp', 'owner'))
- left_new: float32 [32, 1024, 1024], P(('fsdp', 'owner'))
- right_new: float32 [32, 1024, 1024], P(('fsdp', 'owner'))
The draws below stay inside these ranges and needn't reach their ends.
Inputs may be any that keep to these rules, and one draw needn't show every extreme that they name: assign is a permutation of the 32 blocks; slot s holds block assign[s], and each device owns a run of 1 slots. `left_stats`: each block is symmetric positive definite. `right_stats`: each block is symmetric positive definite.
All inputs are finite; a program needn't handle non-finite values.
Results may differ from the reference program's by a relative error of at most 0.001.
The reference program's roundings to bfloat16 on the way count: a program that leaves them out, or rounds other values in their place, can miss the bound.
Values may be sent and summed in bfloat16 or wider, within the bound.
A program may use at most 128 MiB of HBM per device.

```python
import math
import jax
import jax.numpy as jnp
from jax import lax

B = 1024
ITERS = 2
BLOCKS = 32


def decay_table(length):
    places = jnp.arange(B, dtype=jnp.float32)
    distance = jnp.abs(places[:, None] - places[None, :])
    return jnp.exp(-distance / length)


def profile(key, lowest, highest):
    size_key, sign_key = jax.random.split(key)
    magnitude = jnp.exp(jax.random.uniform(size_key, (BLOCKS, B), jnp.float32, math.log(lowest), math.log(highest)))
    signs = jax.random.rademacher(sign_key, (BLOCKS, B), jnp.float32)
    return magnitude * signs


def stat_draw(key, lowest, highest, floor_low, floor_high, length):
    first_key, second_key = jax.random.split(key)
    scales = profile(first_key, lowest, highest)
    floor = jnp.exp(jax.random.uniform(second_key, (BLOCKS, B), jnp.float32, math.log(floor_low), math.log(floor_high)))
    identity = jnp.eye(B, dtype=jnp.float32)
    kernel = 0.1 * scales[:, :, None] * scales[:, None, :] * decay_table(length)[None, :, :]
    return kernel + floor[:, :, None] * identity


def grad_draw(key, lowest, highest, weight, length, noise):
    row_key, col_key = jax.random.split(key)
    rows = profile(row_key, lowest, highest)
    cols = profile(col_key, lowest, highest)
    smooth = weight * rows[:, :, None] * cols[:, None, :] * decay_table(length)[None, :, :]
    return ((smooth + noise) / math.sqrt(B)).astype(jnp.bfloat16)


def draw_grads(key, part):
    key = jax.random.fold_in(key, 21)
    shape_key, noise_key = jax.random.split(key)
    noise = jnp.clip(jax.random.normal(noise_key, (BLOCKS, B, B), jnp.float32), -4.0, 4.0)
    return grad_draw(shape_key, 0.3, 3.0, 4.0, B / 32.0, noise)


def draw_left_stats(key, part):
    key = jax.random.fold_in(key, 11)
    return stat_draw(key, 0.3, 3.0, 0.05, 0.5, B / 32.0)


def draw_right_stats(key, part):
    key = jax.random.fold_in(key, 12)
    return stat_draw(key, 0.3, 3.0, 0.05, 0.5, B / 32.0)


def shard_levels(key, shape, cuts, least, largest):
    loudness = 1.0
    for position, parts in cuts:
        heights = jax.random.uniform(jax.random.fold_in(jax.random.fold_in(key, 6), position), (parts,), jnp.float32, least / len(cuts), largest / len(cuts))
        loudness = loudness * jnp.repeat(jnp.exp(heights), shape[position] // parts).reshape((-1,) + (1,) * (len(shape) - 1 - position))
    return loudness


def setup_inputs(seed: int = 0) -> dict:
    key_list = jax.random.split(jax.random.key(seed), 6)
    return {
        "grads": draw_grads(jax.random.fold_in(key_list[5], 71), 0),
        "second_moment": jnp.clip(jnp.exp(math.log(0.00390625) - 2.7725887 * jax.random.uniform(key_list[1], (BLOCKS, B, B), jnp.float32) ** shard_levels(key_list[1], (BLOCKS, B, B), ((1, 32),), -0.2, 0.2)), 0.00024414062, 0.00390625),
        "assign": jax.random.permutation(key_list[2], BLOCKS).astype(jnp.int32),
        "left_stats": draw_left_stats(jax.random.fold_in(key_list[5], 71), 0),
        "right_stats": draw_right_stats(jax.random.fold_in(key_list[5], 71), 0),
    }


def inverse_root(factor):
    dimension = factor.shape[0]
    identity = jnp.eye(dimension, dtype=jnp.float32)
    frob_norm = jnp.sqrt(jnp.sum(factor * factor))
    ns_matrix = factor / frob_norm
    root_now = identity
    for sweep in range(ITERS):
        newton_mix = (5.0 * identity - ns_matrix) * 0.25
        mix_low = newton_mix.astype(jnp.bfloat16)
        if sweep == 0:
            root_now = frob_norm ** (-0.25) * newton_mix
        else:
            root_now = jnp.dot(root_now.astype(jnp.bfloat16), mix_low, preferred_element_type=jnp.float32)
        if sweep < ITERS - 1:
            square = jnp.dot(mix_low, mix_low, preferred_element_type=jnp.float32).astype(jnp.bfloat16)
            fourth = jnp.dot(square, square, preferred_element_type=jnp.float32).astype(jnp.bfloat16)
            ns_matrix = jnp.dot(fourth, ns_matrix.astype(jnp.bfloat16), preferred_element_type=jnp.float32)
    return root_now.astype(jnp.bfloat16)

def owner_update(grad_block, left_stat, right_stat, adam_sq):
    identity = jnp.eye(grad_block.shape[0], dtype=jnp.float32)
    left_full = 0.9 * left_stat + 0.1 * jnp.dot(grad_block, grad_block.T, preferred_element_type=jnp.float32) + 0.0001 * identity
    right_full = 0.9 * right_stat + 0.1 * jnp.dot(grad_block.T, grad_block, preferred_element_type=jnp.float32) + 0.0001 * identity
    left_root = inverse_root(left_full)
    right_root = inverse_root(right_full)
    left_applied = jnp.dot(left_root, grad_block, preferred_element_type=jnp.float32).astype(jnp.bfloat16)
    precond = jnp.dot(left_applied, right_root, preferred_element_type=jnp.float32)
    precond_sq = jnp.mean(precond * precond)
    precond_low = lax.optimization_barrier(precond.astype(jnp.bfloat16))
    scaled = precond_low.astype(jnp.float32) * (jnp.sqrt(adam_sq) / jnp.sqrt(precond_sq + 1e-06))
    return (scaled.astype(jnp.bfloat16), left_full, right_full)

def reference(grads, second_moment, assign, left_stats, right_stats):

    def slot_work(slot_item):
        block_index, left_stat, right_stat = slot_item
        grad_block = grads[block_index]
        grad_wide = grad_block.astype(jnp.float32)
        moment = 0.9 * second_moment[block_index] + 0.1 * grad_wide * grad_wide
        adam_dir = grad_wide / (jnp.sqrt(moment) + 1e-08)
        adam_sq = jnp.mean(adam_dir * adam_dir)
        return owner_update(grad_block, left_stat, right_stat, adam_sq)
    slot_updates, left_new, right_new = lax.map(slot_work, (assign, left_stats, right_stats))
    update = jnp.zeros_like(grads).at[assign].set(slot_updates)
    return (update, left_new, right_new)
```

```python
import functools

import jax
import jax.numpy as jnp
from jax import lax
from jax.experimental import pallas as pl
from jax.experimental.pallas import tpu as pltpu
from jax.sharding import PartitionSpec as P

MESH = pl.DeviceIdType.MESH
ANY = pl.BlockSpec(memory_space=pl.ANY)
VMEM = pl.BlockSpec(memory_space=pltpu.VMEM)
SMEM = pl.BlockSpec(memory_space=pltpu.SMEM)
F32 = jnp.float32
BF16 = jnp.bfloat16


def dot(a, b):
    return jnp.dot(a, b, preferred_element_type=F32)


def peer_at(fsdp_count, owner_count, step):
    fsdp_off = lax.rem(step // owner_count + fsdp_count // 2, fsdp_count)
    owner_off = lax.rem(step, owner_count)
    fsdp = lax.rem(lax.axis_index("fsdp") + fsdp_off, fsdp_count)
    owner = lax.rem(lax.axis_index("owner") + owner_off, owner_count)
    return fsdp, owner


def exchange(fsdp_count, owner_count, x_ref, o_ref, send_sem, recv_sem, own_sem, between):
    count = fsdp_count * owner_count
    me = lax.axis_index("fsdp") * owner_count + lax.axis_index("owner")
    own_step = (fsdp_count - fsdp_count // 2) * owner_count

    def others(action):
        def body(step, carry):
            action(step)
            return carry

        lax.fori_loop(0, own_step, body, 0)
        lax.fori_loop(own_step + 1, count, body, 0)

    def copy(step):
        fsdp, owner = peer_at(fsdp_count, owner_count, step)
        return pltpu.make_async_remote_copy(
            src_ref=x_ref.at[fsdp * owner_count + owner],
            dst_ref=o_ref.at[me],
            send_sem=send_sem.at[step],
            recv_sem=recv_sem.at[step],
            device_id=(fsdp, owner),
            device_id_type=MESH,
        )

    barrier = pltpu.get_barrier_semaphore()

    def greet(step):
        pl.semaphore_signal(
            barrier, inc=1, device_id=peer_at(fsdp_count, owner_count, step), device_id_type=MESH
        )

    others(greet)
    own = pltpu.make_async_copy(x_ref.at[me], o_ref.at[me], own_sem)
    own.start()
    pl.semaphore_wait(barrier, count - 1)
    others(lambda step: copy(step).start())
    between()
    own.wait()
    others(lambda step: copy(step).wait())


def gather_kernel(
    fsdp_count, owner_count, x_ref, g_hbm, m_hbm, o_ref, sums_ref,
    g_ref, m_ref, send_sem, recv_sem, own_sem, load_sem,
):
    loads = [
        pltpu.make_async_copy(g_hbm, g_ref, load_sem.at[0]),
        pltpu.make_async_copy(m_hbm, m_ref, load_sem.at[1]),
    ]
    for load in loads:
        load.start()

    def adam():
        for load in loads:
            load.wait()

        def body(block, carry):
            wide = g_ref[block].astype(F32)
            moment = 0.9 * m_ref[block] + 0.1 * wide * wide
            adam_dir = wide / (jnp.sqrt(moment) + 1e-08)
            row = jnp.sum(adam_dir * adam_dir, axis=0, keepdims=True)
            sums_ref[pl.ds(block, 1), :] = row
            return carry

        lax.fori_loop(0, g_ref.shape[0], body, 0)

    exchange(fsdp_count, owner_count, x_ref, o_ref, send_sem, recv_sem, own_sem, adam)


def return_kernel(fsdp_count, owner_count, x_ref, o_ref, send_sem, recv_sem, own_sem):
    exchange(
        fsdp_count, owner_count, x_ref, o_ref, send_sem, recv_sem, own_sem, lambda: None
    )


def exchange_scratch(count):
    return [
        pltpu.SemaphoreType.DMA((count,)),
        pltpu.SemaphoreType.DMA((count,)),
        pltpu.SemaphoreType.DMA,
    ]


def gather_rows(outgoing, grads, second_moment, fsdp_count, owner_count):
    count = fsdp_count * owner_count
    return pl.pallas_call(
        functools.partial(gather_kernel, fsdp_count, owner_count),
        out_shape=(
            jax.ShapeDtypeStruct(outgoing.shape, BF16),
            jax.ShapeDtypeStruct((grads.shape[0], grads.shape[2]), F32),
        ),
        in_specs=[ANY, ANY, ANY],
        out_specs=(ANY, VMEM),
        scratch_shapes=[
            pltpu.VMEM(grads.shape, BF16),
            pltpu.VMEM(second_moment.shape, F32),
        ]
        + exchange_scratch(count)
        + [pltpu.SemaphoreType.DMA((2,))],
        compiler_params=pltpu.CompilerParams(
            collective_id=0, has_side_effects=True, vmem_limit_bytes=24 << 20
        ),
        name="gather_rows",
    )(outgoing, grads, second_moment)


def return_rows(blocks, fsdp_count, owner_count):
    return pl.pallas_call(
        functools.partial(return_kernel, fsdp_count, owner_count),
        out_shape=jax.ShapeDtypeStruct(blocks.shape, BF16),
        in_specs=[ANY],
        out_specs=ANY,
        scratch_shapes=exchange_scratch(fsdp_count * owner_count),
        compiler_params=pltpu.CompilerParams(collective_id=1, has_side_effects=True),
        name="return_rows",
    )(blocks)


def owner_kernel(
    g_ref, ls_hbm, rs_hbm, ln_hbm, rn_hbm, out_ref, sq_ref,
    ls, rs, gt, low, mix, square, fourth, root, load_sem, store_sem,
):
    size = g_ref.shape[0]
    tile = size // 2
    tiles = size // tile
    stats = (ls, rs)
    loads = [
        pltpu.make_async_copy(ls_hbm, ls, load_sem.at[0]),
        pltpu.make_async_copy(rs_hbm, rs, load_sem.at[1]),
    ]
    for load in loads:
        load.start()

    def diagonal(step, height):
        rows = lax.broadcasted_iota(jnp.int32, (height, size), 0) + step * height
        cols = lax.broadcasted_iota(jnp.int32, (height, size), 1)
        return rows == cols

    def rows_of(step, height=tile):
        return pl.ds(pl.multiple_of(step * height, height), height)

    gt[...] = g_ref[...].T
    for load in loads:
        load.wait()

    def gram(step, carry):
        here = rows_of(step)
        eye = jnp.where(diagonal(step, tile), 0.0001, 0.0).astype(F32)
        left = 0.9 * ls[here, :] + 0.1 * dot(g_ref[here, :], gt[...]) + eye
        ls[here, :] = left
        right = 0.9 * rs[here, :] + 0.1 * dot(gt[here, :], g_ref[...]) + eye
        rs[here, :] = right
        return (
            carry[0] + jnp.sum(left * left, axis=0, keepdims=True),
            carry[1] + jnp.sum(right * right, axis=0, keepdims=True),
        )

    zero = jnp.zeros((1, size), F32)
    sums = lax.fori_loop(0, tiles, gram, (zero, zero))
    stores = [
        pltpu.make_async_copy(ls, ln_hbm, store_sem.at[0]),
        pltpu.make_async_copy(rs, rn_hbm, store_sem.at[1]),
    ]
    for store in stores:
        store.start()
    frobs = [jnp.sqrt(jnp.sum(total, axis=1, keepdims=True)) for total in sums]
    inverses = [1.0 / frob for frob in frobs]
    scales = [lax.rsqrt(jnp.sqrt(frob)) for frob in frobs]

    def first(step, carry):
        here = rows_of(step, 128)
        eye = jnp.where(diagonal(step, 128), 5.0, 0.0).astype(F32)
        for side in range(2):
            matrix = stats[side][here, :] * inverses[side]
            newton = (eye - matrix) * 0.25
            low[side, here, :] = matrix.astype(BF16)
            mix[side, here, :] = newton.astype(BF16)
            root[side, here, :] = (scales[side] * newton).astype(BF16)
        return carry

    lax.fori_loop(0, size // 128, first, 0)

    def product(a, b, out, finish):
        def body(step, carry):
            here = rows_of(step)
            for side in range(2):
                out[side, here, :] = finish(step, dot(a[side, here, :], b[side])).astype(BF16)
            return carry

        lax.fori_loop(0, tiles, body, 0)

    def as_is(step, value):
        return value

    def newton_mix(step, value):
        return (jnp.where(diagonal(step, tile), 5.0, 0.0).astype(F32) - value) * 0.25

    product(mix, mix, square, as_is)
    product(square, square, fourth, as_is)
    product(fourth, low, mix, newton_mix)
    product(root, mix, square, as_is)

    def apply_left(step, carry):
        here = rows_of(step)
        gt[here, :] = dot(square[0, here, :], g_ref[...]).astype(BF16)
        return carry

    lax.fori_loop(0, tiles, apply_left, 0)

    def apply_right(step, carry):
        here = rows_of(step)
        value = dot(gt[here, :], square[1])
        out_ref[here, :] = value.astype(BF16)
        return carry + jnp.sum(value * value, axis=0, keepdims=True)

    sq_ref[...] = lax.fori_loop(0, tiles, apply_right, zero)
    for store in stores:
        store.wait()


def owner_update(block, left_stat, right_stat):
    shape = block.shape
    pair = (2,) + shape
    return pl.pallas_call(
        owner_kernel,
        out_shape=(
            jax.ShapeDtypeStruct(shape, F32),
            jax.ShapeDtypeStruct(shape, F32),
            jax.ShapeDtypeStruct(shape, BF16),
            jax.ShapeDtypeStruct((1, shape[1]), F32),
        ),
        in_specs=[VMEM, ANY, ANY],
        out_specs=(ANY, ANY, VMEM, VMEM),
        scratch_shapes=[
            pltpu.VMEM(shape, F32),
            pltpu.VMEM(shape, F32),
            pltpu.VMEM(shape, BF16),
            pltpu.VMEM(pair, BF16),
            pltpu.VMEM(pair, BF16),
            pltpu.VMEM(pair, BF16),
            pltpu.VMEM(pair, BF16),
            pltpu.VMEM(pair, BF16),
            pltpu.SemaphoreType.DMA((2,)),
            pltpu.SemaphoreType.DMA((2,)),
        ],
        compiler_params=pltpu.CompilerParams(vmem_limit_bytes=56 << 20),
        name="owner_update",
    )(block, left_stat, right_stat)


def place_kernel(assign_ref, level_ref, x_ref, o_ref):
    count = x_ref.shape[0]

    def body(slot, carry):
        block = assign_ref[slot]
        scale = level_ref[block] * level_ref[count + slot]
        o_ref[block] = (x_ref[slot].astype(F32) * scale).astype(BF16)
        return carry

    lax.fori_loop(0, count, body, 0)


def place_rows(assign, levels, arrived):
    return pl.pallas_call(
        place_kernel,
        out_shape=jax.ShapeDtypeStruct(arrived.shape, BF16),
        in_specs=[SMEM, SMEM, VMEM],
        out_specs=VMEM,
        compiler_params=pltpu.CompilerParams(vmem_limit_bytes=24 << 20),
        name="place_rows",
    )(assign, levels, arrived)


def local(fsdp_count, owner_count, grads, second_moment, assign, left_stats, right_stats):
    count = fsdp_count * owner_count
    size = grads.shape[2]
    me = lax.axis_index("fsdp") * owner_count + lax.axis_index("owner")
    received, sums = gather_rows(grads[assign], grads, second_moment, fsdp_count, owner_count)
    left_new, right_new, precond_low, squares = owner_update(
        received.reshape(size, size), left_stats[0], right_stats[0]
    )
    arrived = return_rows(precond_low.reshape(grads.shape), fsdp_count, owner_count)
    mine = jnp.where(jnp.arange(count) == me, jnp.sum(squares), 0.0)
    totals = lax.psum(jnp.concatenate([jnp.sum(sums, axis=1), mine]), ("fsdp", "owner"))
    means = totals / (size * size)
    levels = jnp.where(
        jnp.arange(2 * count) < count, jnp.sqrt(means), 1.0 / jnp.sqrt(means + 1e-06)
    )
    update = place_rows(assign, levels, arrived)
    return (update, left_new[None], right_new[None])


def solution(mesh):
    rows = P(None, ("fsdp", "owner"), None)
    blocks = P(("fsdp", "owner"), None, None)
    return jax.shard_map(
        functools.partial(local, mesh.shape["fsdp"], mesh.shape["owner"]),
        mesh=mesh,
        in_specs=(rows, rows, P(), blocks, blocks),
        out_specs=(rows, blocks, blocks),
        check_vma=False,
    )
```

```python
import functools
import math

import jax
import jax.numpy as jnp
from jax import lax
from jax.experimental import pallas as pl
from jax.experimental.pallas import tpu as pltpu
from jax.sharding import PartitionSpec as P

MESH = pl.DeviceIdType.MESH
ANY = pl.BlockSpec(memory_space=pl.ANY)
VMEM = pl.BlockSpec(memory_space=pltpu.VMEM)
SMEM = pl.BlockSpec(memory_space=pltpu.SMEM)
F32 = jnp.float32
BF16 = jnp.bfloat16
VMEM_BYTES = 56 << 20


def dot(a, b):
    return jnp.dot(a, b, preferred_element_type=F32)


def peers(fsdp_count, owner_count):
    half = fsdp_count // 2
    stride = next(k for k in range(half + 1, 2 * fsdp_count) if math.gcd(k, fsdp_count) == 1)
    fsdp, owner = lax.axis_index("fsdp"), lax.axis_index("owner")

    def wrap(value, count):
        return jnp.where(value >= count, value - count, value)

    for step in range(fsdp_count * owner_count):
        inner = step % fsdp_count
        fsdp_off = (half + stride * inner) % fsdp_count
        owner_off = (step // fsdp_count + inner) % owner_count
        if fsdp_off or owner_off:
            yield wrap(fsdp + fsdp_off, fsdp_count), wrap(owner + owner_off, owner_count)


def position(owner_count):
    return lax.axis_index("fsdp") * owner_count + lax.axis_index("owner")


def send_all(fsdp_count, owner_count, x_ref, o_ref, send_sem, recv_sem):
    me = position(owner_count)
    for fsdp, owner in peers(fsdp_count, owner_count):
        pltpu.make_async_remote_copy(
            src_ref=x_ref.at[fsdp * owner_count + owner],
            dst_ref=o_ref.at[me],
            send_sem=send_sem,
            recv_sem=recv_sem,
            device_id=(fsdp, owner),
            device_id_type=MESH,
        ).start()


def wait_all(x_ref, o_ref, send_sem, recv_sem):
    most = pl.ds(0, o_ref.shape[0] - 1)
    pltpu.make_async_copy(o_ref.at[most], o_ref.at[most], recv_sem).wait()
    pltpu.make_async_copy(x_ref.at[most], x_ref.at[most], send_sem).wait()


def greet_all(fsdp_count, owner_count):
    barrier = pltpu.get_barrier_semaphore()
    for peer in peers(fsdp_count, owner_count):
        pl.semaphore_signal(barrier, inc=1, device_id=peer, device_id_type=MESH)


def greeted(fsdp_count, owner_count):
    pl.semaphore_wait(pltpu.get_barrier_semaphore(), fsdp_count * owner_count - 1)


def gather_kernel(
    fsdp_count, owner_count, g_hbm, m_hbm, assign_ref, o_ref, parts_ref,
    g_ref, m_ref, out_ref, sums, stage, row_sem, part_sem, own_sem, load_sem,
):
    me = position(owner_count)
    load_g = pltpu.make_async_copy(g_hbm, g_ref, load_sem.at[0])
    load_m = pltpu.make_async_copy(m_hbm, m_ref, load_sem.at[1])
    load_g.start()
    load_m.start()
    greet_all(fsdp_count, owner_count)
    count, row_count, width = g_ref.shape
    load_g.wait()

    def rows_by_slot(slot, carry):
        out_ref[slot] = g_ref[assign_ref[slot]]
        return carry

    lax.fori_loop(0, count, rows_by_slot, 0)
    own = pltpu.make_async_copy(out_ref.at[me], o_ref.at[me], own_sem.at[0])
    own.start()
    greeted(fsdp_count, owner_count)
    send_all(fsdp_count, owner_count, out_ref, o_ref, row_sem.at[0], row_sem.at[1])
    load_m.wait()

    def adam(block, carry):
        wide = g_ref[block].astype(F32)
        moment = 0.9 * m_ref[block] + 0.1 * wide * wide
        adam_dir = wide / (jnp.sqrt(moment) + 1e-08)
        folded = jnp.sum((adam_dir * adam_dir).reshape(row_count // 8, 8, width), axis=0)
        sums[block] = sum(folded[:, at : at + 128] for at in range(0, width, 128))
        return carry

    lax.fori_loop(0, count, adam, 0)

    def parts_by_slot(slot, carry):
        stage[slot] = sums[assign_ref[slot]]
        return carry

    lax.fori_loop(0, count, parts_by_slot, 0)
    own_part = pltpu.make_async_copy(stage.at[me], parts_ref.at[me], own_sem.at[1])
    own_part.start()
    send_all(fsdp_count, owner_count, stage, parts_ref, part_sem.at[0], part_sem.at[1])
    own.wait()
    own_part.wait()
    wait_all(out_ref, o_ref, row_sem.at[0], row_sem.at[1])
    wait_all(stage, parts_ref, part_sem.at[0], part_sem.at[1])


def return_kernel(fsdp_count, owner_count, x_ref, o_ref, row_sem, own_sem):
    me = position(owner_count)
    greet_all(fsdp_count, owner_count)
    own = pltpu.make_async_copy(x_ref.at[me], o_ref.at[me], own_sem)
    own.start()
    greeted(fsdp_count, owner_count)
    send_all(fsdp_count, owner_count, x_ref, o_ref, row_sem.at[0], row_sem.at[1])
    own.wait()
    wait_all(x_ref, o_ref, row_sem.at[0], row_sem.at[1])


def gather_rows(grads, second_moment, assign, fsdp_count, owner_count):
    count = fsdp_count * owner_count
    part = (count, 8, 128)
    return pl.pallas_call(
        functools.partial(gather_kernel, fsdp_count, owner_count),
        out_shape=(
            jax.ShapeDtypeStruct(grads.shape, BF16),
            jax.ShapeDtypeStruct(part, F32),
        ),
        in_specs=[ANY, ANY, SMEM],
        out_specs=(ANY, ANY),
        scratch_shapes=[
            pltpu.VMEM(grads.shape, BF16),
            pltpu.VMEM(second_moment.shape, F32),
            pltpu.VMEM(grads.shape, BF16),
            pltpu.VMEM(part, F32),
            pltpu.VMEM(part, F32),
            pltpu.SemaphoreType.DMA((2,)),
            pltpu.SemaphoreType.DMA((2,)),
            pltpu.SemaphoreType.DMA((2,)),
            pltpu.SemaphoreType.DMA((2,)),
        ],
        compiler_params=pltpu.CompilerParams(
            collective_id=0, has_side_effects=True, vmem_limit_bytes=VMEM_BYTES
        ),
        name="gather_rows",
    )(grads, second_moment, assign)


def return_rows(blocks, fsdp_count, owner_count):
    return pl.pallas_call(
        functools.partial(return_kernel, fsdp_count, owner_count),
        out_shape=jax.ShapeDtypeStruct(blocks.shape, BF16),
        in_specs=[ANY],
        out_specs=ANY,
        scratch_shapes=[
            pltpu.SemaphoreType.DMA((2,)),
            pltpu.SemaphoreType.DMA,
        ],
        compiler_params=pltpu.CompilerParams(
            collective_id=1, has_side_effects=True, vmem_limit_bytes=VMEM_BYTES
        ),
        name="return_rows",
    )(blocks)


def scatter_kernel(assign_ref, x_ref, o_ref, held, load_sem, store_sem):
    def load(slot):
        return pltpu.make_async_copy(x_ref.at[slot], held.at[slot], load_sem.at[slot])

    def store(slot):
        return pltpu.make_async_copy(
            held.at[slot], o_ref.at[assign_ref[slot]], store_sem.at[slot]
        )

    def fill(slot, carry):
        load(slot).start()
        return carry

    def turn(slot, carry):
        load(slot).wait()
        store(slot).start()
        return carry

    def drain(slot, carry):
        store(slot).wait()
        return carry

    for body in (fill, turn, drain):
        lax.fori_loop(0, x_ref.shape[0], body, 0)


def scatter_rows(assign, x):
    return pl.pallas_call(
        scatter_kernel,
        out_shape=jax.ShapeDtypeStruct(x.shape, x.dtype),
        in_specs=[SMEM, ANY],
        out_specs=ANY,
        scratch_shapes=[
            pltpu.VMEM(x.shape, x.dtype),
            pltpu.SemaphoreType.DMA((x.shape[0],)),
            pltpu.SemaphoreType.DMA((x.shape[0],)),
        ],
        compiler_params=pltpu.CompilerParams(vmem_limit_bytes=VMEM_BYTES),
        name="scatter_rows",
    )(assign, x)


def owner_kernel(
    g_ref, ls_hbm, rs_hbm, parts_ref, ln_hbm, rn_hbm, out_ref,
    ls, rs, gt, low, mix, square, fourth, root, precond, load_sem, store_sem,
):
    size = g_ref.shape[0]
    tile = size // 2
    tiles = size // tile
    stats = (ls, rs)
    loads = [
        pltpu.make_async_copy(ls_hbm, ls, load_sem.at[0]),
        pltpu.make_async_copy(rs_hbm, rs, load_sem.at[1]),
    ]
    for load in loads:
        load.start()

    def diagonal(step, height):
        rows = lax.broadcasted_iota(jnp.int32, (height, size), 0) + step * height
        cols = lax.broadcasted_iota(jnp.int32, (height, size), 1)
        return rows == cols

    def rows_of(step, height=tile):
        return pl.ds(pl.multiple_of(step * height, height), height)

    gt[...] = g_ref[...].T
    for load in loads:
        load.wait()

    def gram(step, carry):
        here = rows_of(step)
        eye = jnp.where(diagonal(step, tile), 0.0001, 0.0).astype(F32)
        left = 0.9 * ls[here, :] + 0.1 * dot(g_ref[here, :], gt[...]) + eye
        ls[here, :] = left
        right = 0.9 * rs[here, :] + 0.1 * dot(gt[here, :], g_ref[...]) + eye
        rs[here, :] = right
        return (
            carry[0] + jnp.sum(left * left, axis=0, keepdims=True),
            carry[1] + jnp.sum(right * right, axis=0, keepdims=True),
        )

    zero = jnp.zeros((1, size), F32)
    sums = lax.fori_loop(0, tiles, gram, (zero, zero))
    stores = [
        pltpu.make_async_copy(ls, ln_hbm, store_sem.at[0]),
        pltpu.make_async_copy(rs, rn_hbm, store_sem.at[1]),
    ]
    for store in stores:
        store.start()
    frobs = [jnp.sqrt(jnp.sum(total, axis=1, keepdims=True)) for total in sums]
    inverses = [1.0 / frob for frob in frobs]
    scales = [lax.rsqrt(jnp.sqrt(frob)) for frob in frobs]

    def first(step, carry):
        here = rows_of(step, 128)
        eye = jnp.where(diagonal(step, 128), 5.0, 0.0).astype(F32)
        for side in range(2):
            matrix = stats[side][here, :] * inverses[side]
            newton = (eye - matrix) * 0.25
            low[side, here, :] = matrix.astype(BF16)
            mix[side, here, :] = newton.astype(BF16)
            root[side, here, :] = (scales[side] * newton).astype(BF16)
        return carry

    lax.fori_loop(0, size // 128, first, 0)

    def product(a, b, out, finish):
        def body(step, carry):
            here = rows_of(step)
            for side in range(2):
                out[side, here, :] = finish(step, dot(a[side, here, :], b[side])).astype(BF16)
            return carry

        lax.fori_loop(0, tiles, body, 0)

    def as_is(step, value):
        return value

    def newton_mix(step, value):
        return (jnp.where(diagonal(step, tile), 5.0, 0.0).astype(F32) - value) * 0.25

    product(mix, mix, square, as_is)
    product(square, square, fourth, as_is)
    product(fourth, low, mix, newton_mix)
    product(root, mix, square, as_is)

    def apply_left(step, carry):
        here = rows_of(step)
        gt[here, :] = dot(square[0, here, :], g_ref[...]).astype(BF16)
        return carry

    lax.fori_loop(0, tiles, apply_left, 0)

    def apply_right(step, carry):
        here = rows_of(step)
        value = dot(gt[here, :], square[1])
        precond[here, :] = value.astype(BF16)
        return carry + jnp.sum(value * value, axis=0, keepdims=True)

    squares = lax.fori_loop(0, tiles, apply_right, zero)
    precond_sq = jnp.sum(squares, axis=1, keepdims=True) / (size * size)
    parts = jnp.sum(parts_ref[...], axis=0)
    parts = jnp.sum(parts, axis=0, keepdims=True)
    adam_sq = jnp.sum(parts, axis=1, keepdims=True) / (size * size)
    graft = jnp.sqrt(adam_sq) / jnp.sqrt(precond_sq + 1e-06)

    def rescale(step, carry):
        here = rows_of(step, 128)
        out_ref[here, :] = (precond[here, :].astype(F32) * graft).astype(BF16)
        return carry

    lax.fori_loop(0, size // 128, rescale, 0)
    for store in stores:
        store.wait()


def owner_update(block, left_stat, right_stat, parts):
    shape = block.shape
    pair = (2,) + shape
    return pl.pallas_call(
        owner_kernel,
        out_shape=(
            jax.ShapeDtypeStruct(shape, F32),
            jax.ShapeDtypeStruct(shape, F32),
            jax.ShapeDtypeStruct(shape, BF16),
        ),
        in_specs=[VMEM, ANY, ANY, VMEM],
        out_specs=(ANY, ANY, VMEM),
        scratch_shapes=[
            pltpu.VMEM(shape, F32),
            pltpu.VMEM(shape, F32),
            pltpu.VMEM(shape, BF16),
            pltpu.VMEM(pair, BF16),
            pltpu.VMEM(pair, BF16),
            pltpu.VMEM(pair, BF16),
            pltpu.VMEM(pair, BF16),
            pltpu.VMEM(pair, BF16),
            pltpu.VMEM(shape, BF16),
            pltpu.SemaphoreType.DMA((2,)),
            pltpu.SemaphoreType.DMA((2,)),
        ],
        compiler_params=pltpu.CompilerParams(vmem_limit_bytes=VMEM_BYTES),
        name="owner_update",
    )(block, left_stat, right_stat, parts)


def local(fsdp_count, owner_count, grads, second_moment, assign, left_stats, right_stats):
    size = grads.shape[2]
    received, parts = gather_rows(grads, second_moment, assign, fsdp_count, owner_count)
    left_new, right_new, update = owner_update(
        received.reshape(size, size), left_stats[0], right_stats[0], parts
    )
    arrived = return_rows(update.reshape(grads.shape), fsdp_count, owner_count)
    return (scatter_rows(assign, arrived), left_new[None], right_new[None])


def solution(mesh):
    rows = P(None, ("fsdp", "owner"), None)
    blocks = P(("fsdp", "owner"), None, None)
    return jax.shard_map(
        functools.partial(local, mesh.shape["fsdp"], mesh.shape["owner"]),
        mesh=mesh,
        in_specs=(rows, rows, P(), blocks, blocks),
        out_specs=(rows, blocks, blocks),
        check_vma=False,
    )
```

```python
import functools
import math

import jax
import jax.numpy as jnp
from jax import lax
from jax.experimental import pallas as pl
from jax.experimental.pallas import tpu as pltpu
from jax.sharding import PartitionSpec as P

MESH = pl.DeviceIdType.MESH
ANY = pl.BlockSpec(memory_space=pl.ANY)
VMEM = pl.BlockSpec(memory_space=pltpu.VMEM)
SMEM = pl.BlockSpec(memory_space=pltpu.SMEM)
F32 = jnp.float32
BF16 = jnp.bfloat16
VMEM_BYTES = 56 << 20
TILES = 1
PIECE = 256
CHUNK = 32


def dot(a, b):
    return jnp.dot(a, b, preferred_element_type=F32)


def peers(fsdp_count, owner_count):
    half = fsdp_count // 2
    stride = next(k for k in range(half + 1, 2 * fsdp_count) if math.gcd(k, fsdp_count) == 1)
    fsdp, owner = lax.axis_index("fsdp"), lax.axis_index("owner")

    def wrap(value, count):
        return jnp.where(value >= count, value - count, value)

    for step in range(fsdp_count * owner_count):
        inner = step % fsdp_count
        fsdp_off = (half + stride * inner) % fsdp_count
        owner_off = (step // fsdp_count + inner) % owner_count
        if fsdp_off or owner_off:
            yield wrap(fsdp + fsdp_off, fsdp_count), wrap(owner + owner_off, owner_count)


def position(owner_count):
    return lax.axis_index("fsdp") * owner_count + lax.axis_index("owner")


def send_all(fsdp_count, owner_count, x_ref, o_ref, send_sem, recv_sem):
    me = position(owner_count)
    for fsdp, owner in peers(fsdp_count, owner_count):
        pltpu.make_async_remote_copy(
            src_ref=x_ref.at[fsdp * owner_count + owner],
            dst_ref=o_ref.at[me],
            send_sem=send_sem,
            recv_sem=recv_sem,
            device_id=(fsdp, owner),
            device_id_type=MESH,
        ).start()


def wait_all(x_ref, o_ref, send_sem, recv_sem):
    most = pl.ds(0, o_ref.shape[0] - 1)
    pltpu.make_async_copy(o_ref.at[most], o_ref.at[most], recv_sem).wait()
    pltpu.make_async_copy(x_ref.at[most], x_ref.at[most], send_sem).wait()


def greet_all(fsdp_count, owner_count):
    barrier = pltpu.get_barrier_semaphore()
    for peer in peers(fsdp_count, owner_count):
        pl.semaphore_signal(barrier, inc=1, device_id=peer, device_id_type=MESH)


def greeted(fsdp_count, owner_count):
    pl.semaphore_wait(pltpu.get_barrier_semaphore(), fsdp_count * owner_count - 1)


def gather_kernel(
    fsdp_count, owner_count, g_hbm, m_hbm, assign_ref, o_ref, parts_ref,
    g_ref, m_ref, out_ref, sums, stage, row_sem, part_sem, own_sem, load_sem,
):
    me = position(owner_count)
    load_g = pltpu.make_async_copy(g_hbm, g_ref, load_sem.at[0])
    load_m = pltpu.make_async_copy(m_hbm, m_ref, load_sem.at[1])
    load_g.start()
    load_m.start()
    greet_all(fsdp_count, owner_count)
    count, row_count, width = g_ref.shape
    load_g.wait()

    def rows_by_slot(slot, carry):
        out_ref[slot] = g_ref[assign_ref[slot]]
        return carry

    lax.fori_loop(0, count, rows_by_slot, 0)
    own = pltpu.make_async_copy(out_ref.at[me], o_ref.at[me], own_sem.at[0])
    own.start()
    greeted(fsdp_count, owner_count)
    send_all(fsdp_count, owner_count, out_ref, o_ref, row_sem.at[0], row_sem.at[1])
    load_m.wait()

    def adam(block, carry):
        wide = g_ref[block].astype(F32)
        moment = 0.9 * m_ref[block] + 0.1 * wide * wide
        adam_dir = wide / (jnp.sqrt(moment) + 1e-08)
        folded = jnp.sum((adam_dir * adam_dir).reshape(row_count // 8, 8, width), axis=0)
        sums[block] = sum(folded[:, at : at + 128] for at in range(0, width, 128))
        return carry

    lax.fori_loop(0, count, adam, 0)

    def parts_by_slot(slot, carry):
        stage[slot] = sums[assign_ref[slot]]
        return carry

    lax.fori_loop(0, count, parts_by_slot, 0)
    own_part = pltpu.make_async_copy(stage.at[me], parts_ref.at[me], own_sem.at[1])
    own_part.start()
    send_all(fsdp_count, owner_count, stage, parts_ref, part_sem.at[0], part_sem.at[1])
    own.wait()
    own_part.wait()
    wait_all(out_ref, o_ref, row_sem.at[0], row_sem.at[1])
    wait_all(stage, parts_ref, part_sem.at[0], part_sem.at[1])


def return_kernel(fsdp_count, owner_count, x_ref, o_ref, row_sem, own_sem):
    me = position(owner_count)
    greet_all(fsdp_count, owner_count)
    own = pltpu.make_async_copy(x_ref.at[me], o_ref.at[me], own_sem)
    own.start()
    greeted(fsdp_count, owner_count)
    send_all(fsdp_count, owner_count, x_ref, o_ref, row_sem.at[0], row_sem.at[1])
    own.wait()
    wait_all(x_ref, o_ref, row_sem.at[0], row_sem.at[1])


def gather_rows(grads, second_moment, assign, fsdp_count, owner_count):
    count = fsdp_count * owner_count
    part = (count, 8, 128)
    return pl.pallas_call(
        functools.partial(gather_kernel, fsdp_count, owner_count),
        out_shape=(
            jax.ShapeDtypeStruct(grads.shape, BF16),
            jax.ShapeDtypeStruct(part, F32),
        ),
        in_specs=[ANY, ANY, SMEM],
        out_specs=(ANY, ANY),
        scratch_shapes=[
            pltpu.VMEM(grads.shape, BF16),
            pltpu.VMEM(second_moment.shape, F32),
            pltpu.VMEM(grads.shape, BF16),
            pltpu.VMEM(part, F32),
            pltpu.VMEM(part, F32),
            pltpu.SemaphoreType.DMA((2,)),
            pltpu.SemaphoreType.DMA((2,)),
            pltpu.SemaphoreType.DMA((2,)),
            pltpu.SemaphoreType.DMA((2,)),
        ],
        compiler_params=pltpu.CompilerParams(
            collective_id=0, has_side_effects=True, vmem_limit_bytes=VMEM_BYTES
        ),
        name="gather_rows",
    )(grads, second_moment, assign)


def return_rows(blocks, fsdp_count, owner_count):
    return pl.pallas_call(
        functools.partial(return_kernel, fsdp_count, owner_count),
        out_shape=jax.ShapeDtypeStruct(blocks.shape, BF16),
        in_specs=[ANY],
        out_specs=ANY,
        scratch_shapes=[
            pltpu.SemaphoreType.DMA((2,)),
            pltpu.SemaphoreType.DMA,
        ],
        compiler_params=pltpu.CompilerParams(
            collective_id=1, has_side_effects=True, vmem_limit_bytes=VMEM_BYTES
        ),
        name="return_rows",
    )(blocks)


def scatter_kernel(assign_ref, x_ref, o_ref, held, load_sem, store_sem):
    def load(slot):
        return pltpu.make_async_copy(x_ref.at[slot], held.at[slot], load_sem.at[slot])

    def store(slot):
        return pltpu.make_async_copy(
            held.at[slot], o_ref.at[assign_ref[slot]], store_sem.at[slot]
        )

    def fill(slot, carry):
        load(slot).start()
        return carry

    def turn(slot, carry):
        load(slot).wait()
        store(slot).start()
        return carry

    def drain(slot, carry):
        store(slot).wait()
        return carry

    for body in (fill, turn, drain):
        lax.fori_loop(0, x_ref.shape[0], body, 0)


def scatter_rows(assign, x):
    return pl.pallas_call(
        scatter_kernel,
        out_shape=jax.ShapeDtypeStruct(x.shape, x.dtype),
        in_specs=[SMEM, ANY],
        out_specs=ANY,
        scratch_shapes=[
            pltpu.VMEM(x.shape, x.dtype),
            pltpu.SemaphoreType.DMA((x.shape[0],)),
            pltpu.SemaphoreType.DMA((x.shape[0],)),
        ],
        compiler_params=pltpu.CompilerParams(vmem_limit_bytes=VMEM_BYTES),
        name="scatter_rows",
    )(assign, x)


def owner_kernel(
    g_ref, ls_hbm, rs_hbm, parts_ref, ln_hbm, rn_hbm, out_ref,
    ls, rs, gt, low, mix, square, fourth, root, precond, load_sem, store_sem,
):
    size = g_ref.shape[0]
    tile = size // TILES
    stats = (ls, rs)
    loads = [
        pltpu.make_async_copy(ls_hbm, ls, load_sem.at[0]),
        pltpu.make_async_copy(rs_hbm, rs, load_sem.at[1]),
    ]
    stores = [
        pltpu.make_async_copy(ls, ln_hbm, store_sem.at[0]),
        pltpu.make_async_copy(rs, rn_hbm, store_sem.at[1]),
    ]
    for load in loads:
        load.start()

    def rows_of(step, height):
        return pl.ds(pl.multiple_of(step * height, height), height)

    def diagonal(start, height, at, width, value):
        rows = lax.broadcasted_iota(jnp.int32, (height, width), 0) + start
        cols = lax.broadcasted_iota(jnp.int32, (height, width), 1) + at
        return jnp.where(rows == cols, value, 0.0).astype(F32)

    def product(a, b, finish):
        def run(step, carry):
            rows = a[rows_of(step, tile), :]
            for at in range(0, size, PIECE):
                carry = finish(step, at, dot(rows, b[:, at : at + PIECE]), carry)
            return carry

        return run

    def keep(out):
        def finish(step, at, value, carry):
            out[rows_of(step, tile), at : at + PIECE] = value.astype(BF16)
            return carry

        return finish

    def newton_mix(out):
        def finish(step, at, value, carry):
            mixed = (diagonal(step * tile, tile, at, PIECE, 5.0) - value) * 0.25
            out[rows_of(step, tile), at : at + PIECE] = mixed.astype(BF16)
            return carry

        return finish

    def statistics(stat):
        def finish(step, at, value, carry):
            here, cols = rows_of(step, tile), slice(at, at + PIECE)
            eye = diagonal(step * tile, tile, at, PIECE, 0.0001)
            new = 0.9 * stat[here, cols] + 0.1 * value + eye
            stat[here, cols] = new
            return carry + jnp.sum((new * new).reshape(tile // 8, 8, PIECE), axis=0)

        return finish

    def stage(*works):
        def body(step, carry):
            return tuple(work(step, part) for work, part in zip(works, carry))

        zero = jnp.zeros((8, PIECE), F32)
        return lax.fori_loop(0, TILES, body, (zero,) * len(works))

    def total(partial):
        return jnp.sum(jnp.sum(partial, axis=0, keepdims=True), axis=1, keepdims=True)

    def first(side, squares):
        frob = jnp.sqrt(total(squares))
        inverse = 1.0 / frob
        scale = lax.rsqrt(jnp.sqrt(frob))

        def run(step, carry):
            for part in range(tile // CHUNK):
                start = step * tile + part * CHUNK
                here = pl.ds(pl.multiple_of(start, CHUNK), CHUNK)
                matrix = stats[side][here, :] * inverse
                newton = (diagonal(start, CHUNK, 0, size, 5.0) - matrix) * 0.25
                low[side, here, :] = matrix.astype(BF16)
                mix[side, here, :] = newton.astype(BF16)
                root[side, here, :] = (scale * newton).astype(BF16)
            return carry

        return run

    gt[...] = g_ref[...].T
    loads[0].wait()
    (left_sq,) = stage(product(g_ref, gt, statistics(ls)))
    stores[0].start()
    loads[1].wait()
    right_sq, _ = stage(product(gt, g_ref, statistics(rs)), first(0, left_sq))
    stores[1].start()
    mixes, lows, roots = ([ref.at[side] for side in range(2)] for ref in (mix, low, root))
    squares, fourths = ([ref.at[side] for side in range(2)] for ref in (square, fourth))
    stage(product(mixes[0], mixes[0], keep(squares[0])), first(1, right_sq))
    stage(
        product(mixes[1], mixes[1], keep(squares[1])),
        product(squares[0], squares[0], keep(fourths[0])),
    )
    stage(
        product(squares[1], squares[1], keep(fourths[1])),
        product(fourths[0], lows[0], newton_mix(mixes[0])),
    )
    stage(
        product(fourths[1], lows[1], newton_mix(mixes[1])),
        product(roots[0], mixes[0], keep(squares[0])),
    )
    stage(
        product(roots[1], mixes[1], keep(squares[1])),
        product(squares[0], g_ref, keep(gt)),
    )

    def last(step, at, value, carry):
        precond[rows_of(step, tile), at : at + PIECE] = value.astype(BF16)
        return carry + jnp.sum((value * value).reshape(tile // 8, 8, PIECE), axis=0)

    (precond_squares,) = stage(product(gt, squares[1], last))
    precond_sq = total(precond_squares) / (size * size)
    adam_sq = total(jnp.sum(parts_ref[...], axis=0)) / (size * size)
    graft = jnp.sqrt(adam_sq) / jnp.sqrt(precond_sq + 1e-06)

    def rescale(step, carry):
        here = rows_of(step, CHUNK)
        out_ref[here, :] = (precond[here, :].astype(F32) * graft).astype(BF16)
        return carry

    lax.fori_loop(0, size // CHUNK, rescale, 0)
    for store in stores:
        store.wait()


def owner_update(block, left_stat, right_stat, parts):
    shape = block.shape
    pair = (2,) + shape
    return pl.pallas_call(
        owner_kernel,
        out_shape=(
            jax.ShapeDtypeStruct(shape, F32),
            jax.ShapeDtypeStruct(shape, F32),
            jax.ShapeDtypeStruct(shape, BF16),
        ),
        in_specs=[VMEM, ANY, ANY, VMEM],
        out_specs=(ANY, ANY, VMEM),
        scratch_shapes=[
            pltpu.VMEM(shape, F32),
            pltpu.VMEM(shape, F32),
            pltpu.VMEM(shape, BF16),
            pltpu.VMEM(pair, BF16),
            pltpu.VMEM(pair, BF16),
            pltpu.VMEM(pair, BF16),
            pltpu.VMEM(pair, BF16),
            pltpu.VMEM(pair, BF16),
            pltpu.VMEM(shape, BF16),
            pltpu.SemaphoreType.DMA((2,)),
            pltpu.SemaphoreType.DMA((2,)),
        ],
        compiler_params=pltpu.CompilerParams(vmem_limit_bytes=VMEM_BYTES),
        name="owner_update",
    )(block, left_stat, right_stat, parts)


def local(fsdp_count, owner_count, grads, second_moment, assign, left_stats, right_stats):
    size = grads.shape[2]
    received, parts = gather_rows(grads, second_moment, assign, fsdp_count, owner_count)
    left_new, right_new, update = owner_update(
        received.reshape(size, size), left_stats[0], right_stats[0], parts
    )
    arrived = return_rows(update.reshape(grads.shape), fsdp_count, owner_count)
    return (scatter_rows(assign, arrived), left_new[None], right_new[None])


def solution(mesh):
    rows = P(None, ("fsdp", "owner"), None)
    blocks = P(("fsdp", "owner"), None, None)
    return jax.shard_map(
        functools.partial(local, mesh.shape["fsdp"], mesh.shape["owner"]),
        mesh=mesh,
        in_specs=(rows, rows, P(), blocks, blocks),
        out_specs=(rows, blocks, blocks),
        check_vma=False,
    )
```

```python
import functools
import math

import jax
import jax.numpy as jnp
from jax import lax
from jax.experimental import pallas as pl
from jax.experimental.pallas import tpu as pltpu
from jax.sharding import PartitionSpec as P

MESH = pl.DeviceIdType.MESH
ANY = pl.BlockSpec(memory_space=pl.ANY)
VMEM = pl.BlockSpec(memory_space=pltpu.VMEM)
SMEM = pl.BlockSpec(memory_space=pltpu.SMEM)
F32 = jnp.float32
BF16 = jnp.bfloat16
VMEM_BYTES = 56 << 20
TILES = 1
PIECE = 256
CHUNK = 32


def dot(a, b):
    return jnp.dot(a, b, preferred_element_type=F32)


def peers(fsdp_count, owner_count):
    half = fsdp_count // 2
    stride = next(k for k in range(half + 1, 2 * fsdp_count) if math.gcd(k, fsdp_count) == 1)
    fsdp, owner = lax.axis_index("fsdp"), lax.axis_index("owner")

    def wrap(value, count):
        return jnp.where(value >= count, value - count, value)

    for step in range(fsdp_count * owner_count):
        inner = step % fsdp_count
        fsdp_off = (half + stride * inner) % fsdp_count
        owner_off = (step // fsdp_count + inner) % owner_count
        if fsdp_off or owner_off:
            yield wrap(fsdp + fsdp_off, fsdp_count), wrap(owner + owner_off, owner_count)


def position(owner_count):
    return lax.axis_index("fsdp") * owner_count + lax.axis_index("owner")


def send_all(fsdp_count, owner_count, x_ref, o_ref, send_sem, recv_sem):
    me = position(owner_count)
    for fsdp, owner in peers(fsdp_count, owner_count):
        pltpu.make_async_remote_copy(
            src_ref=x_ref.at[fsdp * owner_count + owner],
            dst_ref=o_ref.at[me],
            send_sem=send_sem,
            recv_sem=recv_sem,
            device_id=(fsdp, owner),
            device_id_type=MESH,
        ).start()


def wait_all(x_ref, o_ref, send_sem, recv_sem):
    most = pl.ds(0, o_ref.shape[0] - 1)
    pltpu.make_async_copy(o_ref.at[most], o_ref.at[most], recv_sem).wait()
    pltpu.make_async_copy(x_ref.at[most], x_ref.at[most], send_sem).wait()


def greet_all(fsdp_count, owner_count):
    barrier = pltpu.get_barrier_semaphore()
    for peer in peers(fsdp_count, owner_count):
        pl.semaphore_signal(barrier, inc=1, device_id=peer, device_id_type=MESH)


def greeted(fsdp_count, owner_count):
    pl.semaphore_wait(pltpu.get_barrier_semaphore(), fsdp_count * owner_count - 1)


def gather_kernel(
    fsdp_count, owner_count, g_hbm, m_hbm, assign_ref, o_ref, parts_ref,
    g_ref, m_ref, out_ref, sums, stage, row_sem, part_sem, own_sem, load_sem,
):
    me = position(owner_count)
    load_g = pltpu.make_async_copy(g_hbm, g_ref, load_sem.at[0])
    load_m = pltpu.make_async_copy(m_hbm, m_ref, load_sem.at[1])
    load_g.start()
    greet_all(fsdp_count, owner_count)
    count, row_count, width = g_ref.shape
    load_g.wait()
    load_m.start()

    def rows_by_slot(slot, carry):
        out_ref[slot] = g_ref[assign_ref[slot]]
        return carry

    lax.fori_loop(0, count, rows_by_slot, 0)
    own = pltpu.make_async_copy(out_ref.at[me], o_ref.at[me], own_sem.at[0])
    own.start()
    greeted(fsdp_count, owner_count)
    send_all(fsdp_count, owner_count, out_ref, o_ref, row_sem.at[0], row_sem.at[1])
    load_m.wait()

    def adam(block, carry):
        wide = g_ref[block].astype(F32)
        moment = 0.9 * m_ref[block] + 0.1 * wide * wide
        adam_dir = wide / (jnp.sqrt(moment) + 1e-08)
        folded = jnp.sum((adam_dir * adam_dir).reshape(row_count // 8, 8, width), axis=0)
        sums[block] = sum(folded[:, at : at + 128] for at in range(0, width, 128))
        return carry

    lax.fori_loop(0, count, adam, 0)

    def parts_by_slot(slot, carry):
        stage[slot] = sums[assign_ref[slot]]
        return carry

    lax.fori_loop(0, count, parts_by_slot, 0)
    own_part = pltpu.make_async_copy(stage.at[me], parts_ref.at[me], own_sem.at[1])
    own_part.start()
    send_all(fsdp_count, owner_count, stage, parts_ref, part_sem.at[0], part_sem.at[1])
    own.wait()
    own_part.wait()
    wait_all(out_ref, o_ref, row_sem.at[0], row_sem.at[1])
    wait_all(stage, parts_ref, part_sem.at[0], part_sem.at[1])


def return_kernel(fsdp_count, owner_count, x_ref, o_ref, row_sem, own_sem):
    me = position(owner_count)
    greet_all(fsdp_count, owner_count)
    own = pltpu.make_async_copy(x_ref.at[me], o_ref.at[me], own_sem)
    own.start()
    greeted(fsdp_count, owner_count)
    send_all(fsdp_count, owner_count, x_ref, o_ref, row_sem.at[0], row_sem.at[1])
    own.wait()
    wait_all(x_ref, o_ref, row_sem.at[0], row_sem.at[1])


def gather_rows(grads, second_moment, assign, fsdp_count, owner_count):
    count = fsdp_count * owner_count
    part = (count, 8, 128)
    return pl.pallas_call(
        functools.partial(gather_kernel, fsdp_count, owner_count),
        out_shape=(
            jax.ShapeDtypeStruct(grads.shape, BF16),
            jax.ShapeDtypeStruct(part, F32),
        ),
        in_specs=[ANY, ANY, SMEM],
        out_specs=(ANY, ANY),
        scratch_shapes=[
            pltpu.VMEM(grads.shape, BF16),
            pltpu.VMEM(second_moment.shape, F32),
            pltpu.VMEM(grads.shape, BF16),
            pltpu.VMEM(part, F32),
            pltpu.VMEM(part, F32),
            pltpu.SemaphoreType.DMA((2,)),
            pltpu.SemaphoreType.DMA((2,)),
            pltpu.SemaphoreType.DMA((2,)),
            pltpu.SemaphoreType.DMA((2,)),
        ],
        compiler_params=pltpu.CompilerParams(
            collective_id=0, has_side_effects=True, vmem_limit_bytes=VMEM_BYTES
        ),
        name="gather_rows",
    )(grads, second_moment, assign)


def return_rows(blocks, fsdp_count, owner_count):
    return pl.pallas_call(
        functools.partial(return_kernel, fsdp_count, owner_count),
        out_shape=jax.ShapeDtypeStruct(blocks.shape, BF16),
        in_specs=[ANY],
        out_specs=ANY,
        scratch_shapes=[
            pltpu.SemaphoreType.DMA((2,)),
            pltpu.SemaphoreType.DMA,
        ],
        compiler_params=pltpu.CompilerParams(
            collective_id=1, has_side_effects=True, vmem_limit_bytes=VMEM_BYTES
        ),
        name="return_rows",
    )(blocks)


def scatter_kernel(assign_ref, x_ref, o_ref, held, load_sem, store_sem):
    def load(slot):
        return pltpu.make_async_copy(x_ref.at[slot], held.at[slot], load_sem.at[slot])

    def store(slot):
        return pltpu.make_async_copy(
            held.at[slot], o_ref.at[assign_ref[slot]], store_sem.at[slot]
        )

    def fill(slot, carry):
        load(slot).start()
        return carry

    def turn(slot, carry):
        load(slot).wait()
        store(slot).start()
        return carry

    def drain(slot, carry):
        store(slot).wait()
        return carry

    for body in (fill, turn, drain):
        lax.fori_loop(0, x_ref.shape[0], body, 0)


def scatter_rows(assign, x):
    return pl.pallas_call(
        scatter_kernel,
        out_shape=jax.ShapeDtypeStruct(x.shape, x.dtype),
        in_specs=[SMEM, ANY],
        out_specs=ANY,
        scratch_shapes=[
            pltpu.VMEM(x.shape, x.dtype),
            pltpu.SemaphoreType.DMA((x.shape[0],)),
            pltpu.SemaphoreType.DMA((x.shape[0],)),
        ],
        compiler_params=pltpu.CompilerParams(vmem_limit_bytes=VMEM_BYTES),
        name="scatter_rows",
    )(assign, x)


def owner_kernel(
    g_ref, ls_hbm, rs_hbm, parts_ref, ln_hbm, rn_hbm, out_ref,
    ls, rs, gt, low, mix, square, fourth, root, precond, load_sem, store_sem,
):
    size = g_ref.shape[0]
    tile = size // TILES
    stats = (ls, rs)
    loads = [
        pltpu.make_async_copy(ls_hbm, ls, load_sem.at[0]),
        pltpu.make_async_copy(rs_hbm, rs, load_sem.at[1]),
    ]
    stores = [
        pltpu.make_async_copy(ls, ln_hbm, store_sem.at[0]),
        pltpu.make_async_copy(rs, rn_hbm, store_sem.at[1]),
    ]
    for load in loads:
        load.start()

    def rows_of(step, height):
        return pl.ds(pl.multiple_of(step * height, height), height)

    def diagonal(start, height, at, width, value):
        rows = lax.broadcasted_iota(jnp.int32, (height, width), 0) + start
        cols = lax.broadcasted_iota(jnp.int32, (height, width), 1) + at
        return jnp.where(rows == cols, value, 0.0).astype(F32)

    def product(a, b, finish):
        def run(step, carry):
            rows = a[rows_of(step, tile), :]
            for at in range(0, size, PIECE):
                carry = finish(step, at, dot(rows, b[:, at : at + PIECE]), carry)
            return carry

        return run

    def keep(out):
        def finish(step, at, value, carry):
            out[rows_of(step, tile), at : at + PIECE] = value.astype(BF16)
            return carry

        return finish

    def newton_mix(out):
        def finish(step, at, value, carry):
            mixed = (diagonal(step * tile, tile, at, PIECE, 5.0) - value) * 0.25
            out[rows_of(step, tile), at : at + PIECE] = mixed.astype(BF16)
            return carry

        return finish

    def statistics(stat):
        def finish(step, at, value, carry):
            here, cols = rows_of(step, tile), slice(at, at + PIECE)
            eye = diagonal(step * tile, tile, at, PIECE, 0.0001)
            new = 0.9 * stat[here, cols] + 0.1 * value + eye
            stat[here, cols] = new
            return carry + jnp.sum((new * new).reshape(tile // 8, 8, PIECE), axis=0)

        return finish

    def stage(*works):
        def body(step, carry):
            return tuple(work(step, part) for work, part in zip(works, carry))

        zero = jnp.zeros((8, PIECE), F32)
        return lax.fori_loop(0, TILES, body, (zero,) * len(works))

    def total(partial):
        return jnp.sum(jnp.sum(partial, axis=0, keepdims=True), axis=1, keepdims=True)

    def first(side, squares):
        frob = jnp.sqrt(total(squares))
        inverse = 1.0 / frob
        scale = lax.rsqrt(jnp.sqrt(frob))

        def run(step, carry):
            for part in range(tile // CHUNK):
                start = step * tile + part * CHUNK
                here = pl.ds(pl.multiple_of(start, CHUNK), CHUNK)
                matrix = stats[side][here, :] * inverse
                newton = (diagonal(start, CHUNK, 0, size, 5.0) - matrix) * 0.25
                low[side, here, :] = matrix.astype(BF16)
                mix[side, here, :] = newton.astype(BF16)
                root[side, here, :] = (scale * newton).astype(BF16)
            return carry

        return run

    gt[...] = g_ref[...].T
    loads[0].wait()
    (left_sq,) = stage(product(g_ref, gt, statistics(ls)))
    stores[0].start()
    loads[1].wait()
    right_sq, _ = stage(product(gt, g_ref, statistics(rs)), first(0, left_sq))
    stores[1].start()
    mixes, lows, roots = ([ref.at[side] for side in range(2)] for ref in (mix, low, root))
    squares, fourths = ([ref.at[side] for side in range(2)] for ref in (square, fourth))
    stage(product(mixes[0], mixes[0], keep(squares[0])), first(1, right_sq))
    stage(
        product(mixes[1], mixes[1], keep(squares[1])),
        product(squares[0], squares[0], keep(fourths[0])),
    )
    stage(
        product(squares[1], squares[1], keep(fourths[1])),
        product(fourths[0], lows[0], newton_mix(mixes[0])),
    )
    stage(
        product(fourths[1], lows[1], newton_mix(mixes[1])),
        product(roots[0], mixes[0], keep(squares[0])),
    )
    stage(
        product(roots[1], mixes[1], keep(squares[1])),
        product(squares[0], g_ref, keep(gt)),
    )

    def last(step, at, value, carry):
        precond[rows_of(step, tile), at : at + PIECE] = value.astype(BF16)
        return carry + jnp.sum((value * value).reshape(tile // 8, 8, PIECE), axis=0)

    (precond_squares,) = stage(product(gt, squares[1], last))
    precond_sq = total(precond_squares) / (size * size)
    adam_sq = total(jnp.sum(parts_ref[...], axis=0)) / (size * size)
    graft = jnp.sqrt(adam_sq) / jnp.sqrt(precond_sq + 1e-06)

    def rescale(step, carry):
        here = rows_of(step, 4 * CHUNK)
        out_ref[here, :] = (precond[here, :].astype(F32) * graft).astype(BF16)
        return carry

    lax.fori_loop(0, size // (4 * CHUNK), rescale, 0)
    for store in stores:
        store.wait()


def owner_update(block, left_stat, right_stat, parts):
    shape = block.shape
    pair = (2,) + shape
    return pl.pallas_call(
        owner_kernel,
        out_shape=(
            jax.ShapeDtypeStruct(shape, F32),
            jax.ShapeDtypeStruct(shape, F32),
            jax.ShapeDtypeStruct(shape, BF16),
        ),
        in_specs=[VMEM, ANY, ANY, VMEM],
        out_specs=(ANY, ANY, VMEM),
        scratch_shapes=[
            pltpu.VMEM(shape, F32),
            pltpu.VMEM(shape, F32),
            pltpu.VMEM(shape, BF16),
            pltpu.VMEM(pair, BF16),
            pltpu.VMEM(pair, BF16),
            pltpu.VMEM(pair, BF16),
            pltpu.VMEM(pair, BF16),
            pltpu.VMEM(pair, BF16),
            pltpu.VMEM(shape, BF16),
            pltpu.SemaphoreType.DMA((2,)),
            pltpu.SemaphoreType.DMA((2,)),
        ],
        compiler_params=pltpu.CompilerParams(vmem_limit_bytes=VMEM_BYTES),
        name="owner_update",
    )(block, left_stat, right_stat, parts)


def local(fsdp_count, owner_count, grads, second_moment, assign, left_stats, right_stats):
    size = grads.shape[2]
    received, parts = gather_rows(grads, second_moment, assign, fsdp_count, owner_count)
    left_new, right_new, update = owner_update(
        received.reshape(size, size), left_stats[0], right_stats[0], parts
    )
    arrived = return_rows(update.reshape(grads.shape), fsdp_count, owner_count)
    return (scatter_rows(assign, arrived), left_new[None], right_new[None])


def solution(mesh):
    rows = P(None, ("fsdp", "owner"), None)
    blocks = P(("fsdp", "owner"), None, None)
    return jax.shard_map(
        functools.partial(local, mesh.shape["fsdp"], mesh.shape["owner"]),
        mesh=mesh,
        in_specs=(rows, rows, P(), blocks, blocks),
        out_specs=(rows, blocks, blocks),
        check_vma=False,
    )
```
